32 devices in a mesh: groups: 2 (over x), depth: 8 (over z, y), lat: 2 (over core).
Axes of the slice: x: 2, y: 2, z: 4, core: 2. Of those that a mesh axis runs over, the one named last changes fastest.
Arguments:
- absorb: bfloat16 [64, 32, 4096], P('depth', ('groups', 'lat')), parts along dimension 1, may hold values from 0 to 0.35
- emission: bfloat16 [64, 32, 4096], P('depth', ('groups', 'lat')), parts along dimension 1, may hold values from 0.099609375 to 2
- measured: float32 [8, 32, 4096], P(None, ('groups', 'lat')), parts along dimension 1, may hold values from -6 to 6
- camera_view: int32 [8, 1], replicated, may hold values from 0 to 3
- offsets: int32 [4, 64], P(None, 'depth'), may hold values from -32 to 32
- fractions: float32 [4], replicated, may hold values from 0.2 to 0.8
Outputs:
- grad_absorb: float32 [64, 32, 4096], P('depth', ('groups', 'lat')), parts along dimension 1
- grad_emission: float32 [64, 32, 4096], P('depth', ('groups', 'lat')), parts along dimension 1
The draws below stay inside these ranges and needn't reach their ends.
There are 2 independent parts, one for each index of `groups`. The reference program is written for one: setup_inputs(seed, part) draws one part's arguments, and reference() takes and returns one part's arrays. A program takes and returns all parts, laid end to end along the dimension named above; an argument that names none is the same for every part. Nothing has to cross between parts.
Inputs may be any that keep to these rules, and one draw needn't show every extreme that they name: `camera_view`: every view is seen by at least one camera.
All inputs are finite; a program needn't handle non-finite values.
Results may differ from the reference program's by a relative error of at most 0.0003.
Values may be sent and summed in bfloat16 or wider, within the bound.
A program may use at most 192 MiB of HBM per device.

```python
import math
import jax
import jax.numpy as jnp
from jax import lax

COLUMNS = 4096
VIEWS = 4
CAMERAS = 8
SHIFT_MAX = 32
DEPTH_SLICES = 64
ROWS = 16


def draw_absorb(key, part):
    keys = jax.random.split(jax.random.fold_in(key, 17), 5)
    weak_share = 0.5
    is_weak = jax.random.uniform(keys[0], (ROWS,), jnp.float32) < weak_share
    weak_rate = jnp.exp(jax.random.uniform(keys[1], (ROWS,), jnp.float32, math.log(0.3 / DEPTH_SLICES), math.log(1.5 / DEPTH_SLICES)))
    strong_rate = jnp.exp(jax.random.uniform(keys[2], (ROWS,), jnp.float32, math.log(0.02), math.log(0.06)))
    row_decay_factor = jnp.where(is_weak, weak_rate, strong_rate)
    roughness_penalty = jax.random.uniform(keys[3], (DEPTH_SLICES, ROWS, COLUMNS), jnp.float32, 0.5, 1.5)
    sample_locations = jax.random.randint(keys[4], (3,), 0, DEPTH_SLICES)
    pulse_amount = jnp.any(jnp.arange(DEPTH_SLICES)[:, None] == sample_locations[None, :], axis=1)
    pulse_increment = jnp.where(pulse_amount, 0.25, 0.0).astype(jnp.float32)
    sampled_values = row_decay_factor[None, :, None] * roughness_penalty + pulse_increment[:, None, None]
    return sampled_values.astype(jnp.bfloat16)


def touch_ends(entries, own_key, least, high):
    longest = entries.shape.index(max(entries.shape))
    spots = []
    for shift in (0, 1):
        where = [jax.random.randint(jax.random.fold_in(own_key, axis), (), 0, length) for axis, length in enumerate(entries.shape)]
        where[longest] = (where[longest] + shift) % entries.shape[longest]
        spots.append(tuple(where))
    return entries.at[spots[0]].set(least).at[spots[1]].set(high)


def levels(own_key, shape, cuts, smallest, largest):
    gain = 1.0
    for axis_at, blocks in cuts:
        steps = jax.random.uniform(jax.random.fold_in(jax.random.fold_in(own_key, 6), axis_at), (blocks,), jnp.float32, smallest / len(cuts), largest / len(cuts))
        gain = gain * jnp.repeat(jnp.exp(steps), shape[axis_at] // blocks).reshape((-1,) + (1,) * (len(shape) - 1 - axis_at))
    return gain


def different_ones(stream_key, rows, count, top, lift):
    order = jax.random.permutation(jax.random.fold_in(stream_key, 1), count)
    boost = order
    for power in range(3):
        boost = boost * boost // count
    boost = boost * lift // count
    chance = jax.random.randint(jax.random.fold_in(stream_key, 2), (rows, count), 0, 4096) + boost
    sure = jax.random.permutation(jax.random.fold_in(stream_key, 3), rows)[jnp.arange(count) % rows]
    chance = jnp.where(jnp.arange(rows)[:, None] == sure[None, :], 1 << 14, chance)
    priority = chance * count + jnp.arange(count)
    return lax.top_k(priority.astype(jnp.int32), top)[1].astype(jnp.int32)


def normal_values(stream_key, dims, spread, limit, cuts=(), kind=jnp.bfloat16):
    entries = spread * jax.random.normal(stream_key, dims, jnp.float32)
    if cuts:
        entries = entries * levels(stream_key, dims, cuts, -0.22, 0.18)
    return jnp.clip(entries, -limit, limit).astype(kind)


def setup_inputs(seed: int = 0, part: int = 0) -> dict:
    key_of = jax.random.split(jax.random.key(seed), 7)
    part_keys = jax.random.split(jax.random.fold_in(key_of[6], part), 7)
    absorb = draw_absorb(jax.random.fold_in(jax.random.fold_in(key_of[6], part), 71), part)
    emission = jnp.clip(0.099609375 + 1.9003906 * jax.random.uniform(part_keys[1], (DEPTH_SLICES, ROWS, COLUMNS), jnp.float32) ** levels(part_keys[1], (DEPTH_SLICES, ROWS, COLUMNS), ((0, 8), (1, 2)), -0.2, 0.2), 0.099609375, 2.0).astype(jnp.bfloat16)
    measured = normal_values(part_keys[2], (CAMERAS, ROWS, COLUMNS), 1.0, 6.0, ((1, 2),), jnp.float32)
    camera_view = different_ones(key_of[3], CAMERAS, VIEWS, 1, 0)
    offsets = touch_ends(jax.random.randint(key_of[4], (VIEWS, DEPTH_SLICES), -SHIFT_MAX, SHIFT_MAX + 1), jax.random.fold_in(key_of[4], 1), -SHIFT_MAX, SHIFT_MAX).astype(jnp.int32)
    fractions = jnp.clip(jax.random.uniform(key_of[5], (VIEWS,), jnp.float32, 0.2, 0.8), 0.2, 0.8)
    return {"absorb": absorb, "emission": emission, "measured": measured, "camera_view": camera_view, "offsets": offsets, "fractions": fractions}


reg_absorb = 20.0
reg_emit = 0.05


def shear_take(field, lead, step, weight):
    columns = field.shape[2]
    base_cols = jnp.arange(columns, dtype=jnp.int32)
    first_idx = jnp.remainder(base_cols[None, :] + lead[:, None], columns).astype(jnp.int32)
    second_idx = jnp.remainder(first_idx + step, columns).astype(jnp.int32)
    first_full = jnp.broadcast_to(first_idx[:, None, :], field.shape)
    second_full = jnp.broadcast_to(second_idx[:, None, :], field.shape)
    near_val = jnp.take_along_axis(field, first_full, axis=2).astype(jnp.float32)
    far_val = jnp.take_along_axis(field, second_full, axis=2).astype(jnp.float32)
    return (1.0 - weight) * near_val + weight * far_val


def composite(optical, glowing):
    transmit = jnp.exp(-optical)
    radiance = glowing * (1.0 - transmit)

    def forward(running, slices):
        return running * slices[0], running

    def backward(running, slices):
        return slices[1] + slices[0] * running, running

    _, before = lax.scan(forward, jnp.ones_like(optical[0]), (transmit, radiance))
    _, behind = lax.scan(backward, jnp.zeros_like(optical[0]), (transmit, radiance), reverse=True)
    picture = jnp.sum(before * radiance, axis=0)
    return transmit, before, behind, picture


def laplace(field):
    padded = jnp.pad(field.astype(jnp.float32), ((0, 0), (1, 1), (1, 1)))
    center = padded[:, 1:-1, 1:-1]
    return padded[:, 2:, 1:-1] + padded[:, :-2, 1:-1] + padded[:, 1:-1, 2:] + padded[:, 1:-1, :-2] - 4.0 * center


def reference(absorb, emission, measured, camera_view, offsets, fractions):
    pictures = []
    for view_idx in range(VIEWS):
        optical = shear_take(absorb, offsets[view_idx], 1, fractions[view_idx])
        glowing = shear_take(emission, offsets[view_idx], 1, fractions[view_idx])
        pictures.append(composite(optical, glowing)[3])
    pictures = jnp.stack(pictures)
    onehot = (camera_view == jnp.arange(VIEWS, dtype=jnp.int32)[None, :]).astype(jnp.float32)
    per_camera = jnp.einsum("kv,vrc->krc", onehot, pictures, precision=lax.Precision.HIGHEST)
    residual = per_camera - measured
    adjoint = jnp.einsum("kv,krc->vrc", onehot, residual, precision=lax.Precision.HIGHEST)
    total_absorb = jnp.zeros(absorb.shape, jnp.float32)
    total_emit = jnp.zeros(absorb.shape, jnp.float32)
    for view_idx in range(VIEWS):
        optical = shear_take(absorb, offsets[view_idx], 1, fractions[view_idx])
        glowing = shear_take(emission, offsets[view_idx], 1, fractions[view_idx])
        transmit, before, behind, picture = composite(optical, glowing)
        grad_emit = adjoint[view_idx] * before * (1.0 - transmit)
        grad_abs = adjoint[view_idx] * before * transmit * (glowing - behind)
        total_absorb = total_absorb + shear_take(grad_abs, -offsets[view_idx], -1, fractions[view_idx])
        total_emit = total_emit + shear_take(grad_emit, -offsets[view_idx], -1, fractions[view_idx])
    grad_absorb = total_absorb - reg_absorb * laplace(absorb)
    grad_emission = total_emit - reg_emit * laplace(emission)
    return grad_absorb, grad_emission
```

```python
import functools

import jax
import jax.numpy as jnp
from jax import lax
from jax.experimental import pallas as pl
from jax.experimental.pallas import tpu as pltpu
from jax.sharding import PartitionSpec as P

reg_absorb = 20.0
reg_emit = 0.05
shift_max = 32
lanes = 128
vmem = pltpu.CompilerParams(vmem_limit_bytes=48 * 1024 * 1024)
MESH = pl.DeviceIdType.MESH


def tiles(value):
    return [value[:, i * lanes : (i + 1) * lanes] for i in range(value.shape[1] // lanes)]


def advance(parts, amount, lane):
    turned = [pltpu.roll(part, (lanes - amount) & (lanes - 1), axis=1) for part in parts]
    keep = lane < lanes - amount
    return [jnp.where(keep, turned[i], turned[i + 1]) for i in range(len(parts) - 1)]


def fill(field_ref, near_ref, step_ref, z):
    columns = field_ref.shape[2]
    field = field_ref[z].astype(jnp.float32)
    near = pltpu.roll(field, shift_max, axis=1)
    step = pltpu.roll(field, shift_max - 1, axis=1) - near
    near_ref[z, :, :columns] = near
    near_ref[z, :, columns:] = near[:, :lanes]
    step_ref[z, :, :columns] = step
    step_ref[z, :, columns:] = step[:, :lanes]


def sheared(near_ref, step_ref, z, start, width, amount, weight, lane):
    near = near_ref[z, :, pl.ds(start, width + lanes)]
    step = step_ref[z, :, pl.ds(start, width + lanes)]
    return advance(tiles(near + weight * step), amount, lane)


def first_kernel(
    absorb_ref, emit_ref, offs_ref, frac_ref, out_ref, edge_ref, near_a, step_a, near_e, step_e
):
    slices, rows, columns = absorb_ref.shape
    views = frac_ref.shape[0]
    count, piece = out_ref.shape[0], out_ref.shape[4]
    width = 1024
    lower = lax.axis_index("lat") == 0
    for z in range(slices):
        fill(absorb_ref, near_a, step_a, z)
        fill(emit_ref, near_e, step_e, z)
        for f, ref in enumerate((absorb_ref, emit_ref)):
            field = ref[z].astype(jnp.float32)
            edge_ref[f, z : z + 1, :] = jnp.where(lower, field[rows - 1 :], field[:1])
    lane = lax.broadcasted_iota(jnp.int32, (rows, lanes), 1)
    many = width // lanes

    def view_loop(v, _):
        weight = frac_ref[v]

        def chunk_loop(ch, _):
            start = pl.multiple_of(ch * width, width)
            run, light = None, None
            for z in range(slices):
                amount = offs_ref[v, z] + shift_max
                optical = sheared(near_a, step_a, z, start, width, amount, weight, lane)
                glowing = sheared(near_e, step_e, z, start, width, amount, weight, lane)
                trans = [jnp.exp(-o) for o in optical]
                radiance = [g * (1.0 - t) for g, t in zip(glowing, trans)]
                if z == 0:
                    run, light = trans, radiance
                else:
                    light = [l + r * x for l, r, x in zip(light, run, radiance)]
                    run = [r * t for r, t in zip(run, trans)]
            per = piece // lanes
            for i in range(many):
                dest = ch * (width // piece) + i // per
                cols = slice((i % per) * lanes, (i % per + 1) * lanes)
                out_ref[dest, v, 0, :, cols] = run[i]
                out_ref[dest, v, 1, :, cols] = light[i]
            return 0

        return lax.fori_loop(0, columns // width, chunk_loop, 0)

    lax.fori_loop(0, views, view_loop, 0)


def cross_kernel(
    mine_ref, measured_ref, cam_ref, edge_ref, back_ref, rim_ref, got, sent, s1, r1, s2, r2, s3, r3
):
    count, views, _, rows, piece = mine_ref.shape
    cameras = measured_ref.shape[0]
    me = lax.axis_index("depth")
    lat = lax.axis_index("lat")
    barrier = pltpu.get_barrier_semaphore()
    for p in range(1, count):
        pl.semaphore_signal(
            barrier, inc=1, device_id={"depth": lax.rem(me + p, count)}, device_id_type=MESH
        )
    pl.semaphore_signal(barrier, inc=1, device_id={"lat": 1 - lat}, device_id_type=MESH)
    pl.semaphore_wait(barrier, count)

    def out_copy(v, p):
        to = lax.rem(me + p, count)
        return pltpu.make_async_remote_copy(
            src_ref=mine_ref.at[to, v],
            dst_ref=got.at[me, v],
            send_sem=s1.at[v, p],
            recv_sem=r1.at[v, p],
            device_id={"depth": to},
            device_id_type=MESH,
        )

    def ret_copy(v, p):
        to = lax.rem(me + p, count)
        return pltpu.make_async_remote_copy(
            src_ref=sent.at[to, v],
            dst_ref=back_ref.at[me, v],
            send_sem=s2.at[v, p],
            recv_sem=r2.at[v, p],
            device_id={"depth": to},
            device_id_type=MESH,
        )

    for v in range(views):
        for p in range(1, count):
            out_copy(v, p).start()
    rim = pltpu.make_async_remote_copy(
        src_ref=edge_ref, dst_ref=rim_ref, send_sem=s3, recv_sem=r3,
        device_id={"lat": 1 - lat}, device_id_type=MESH,
    )
    rim.start()
    for v in range(views):
        got[me, v] = mine_ref[me, v]
    start = pl.multiple_of(me * piece, piece)
    for v in range(views):
        for p in range(1, count):
            out_copy(v, p).wait_recv()
        fronts = [jnp.ones((rows, piece), jnp.float32)]
        for j in range(count):
            fronts.append(fronts[-1] * got[j, v, 0])
        behind = jnp.zeros((rows, piece), jnp.float32)
        for j in reversed(range(count)):
            sent[j, v, 1] = behind
            behind = got[j, v, 1] + got[j, v, 0] * behind
        adjoint = jnp.zeros((rows, piece), jnp.float32)
        for k in range(cameras):
            seen = jnp.where(cam_ref[k, 0] == v, 1.0, 0.0).astype(jnp.float32)
            adjoint += seen * (behind - measured_ref[k, :, pl.ds(start, piece)])
        for j in range(count):
            sent[j, v, 0] = adjoint * fronts[j]
        for p in range(1, count):
            ret_copy(v, p).start()
        back_ref[me, v] = sent[me, v]
    rim.wait()
    for v in range(views):
        for p in range(1, count):
            out_copy(v, p).wait_send()
            ret_copy(v, p).wait()


def second_kernel(
    absorb_ref, emit_ref, offs_ref, frac_ref, back_ref, rim_ref, ga_ref, ge_ref,
    near_a, step_a, near_e, step_e, grad_a, grad_e, keep,
):
    slices, rows, columns = absorb_ref.shape
    views = frac_ref.shape[0]
    count, piece = back_ref.shape[0], back_ref.shape[4]
    width = min(512, columns)
    lower = lax.axis_index("lat") == 0
    for z in range(slices):
        fill(absorb_ref, near_a, step_a, z)
        fill(emit_ref, near_e, step_e, z)
    lane = lax.broadcasted_iota(jnp.int32, (rows, lanes), 1)
    many = width // lanes
    per = piece // lanes

    def view_loop(v, _):
        weight = frac_ref[v]

        def chunk_loop(ch, _):
            start = pl.multiple_of(ch * width, width)

            def entering(q):
                if piece >= width:
                    first = ch // (piece // width)
                    inner = pl.multiple_of((ch % (piece // width)) * width, width)
                    return tiles(back_ref[first, v, q, :, pl.ds(inner, width)])
                parts = []
                for i in range(many):
                    cols = slice((i % per) * lanes, (i % per + 1) * lanes)
                    parts.append(back_ref[ch * (width // piece) + i // per, v, q, :, cols])
                return parts

            run = entering(0)
            for z in range(slices):
                amount = offs_ref[v, z] + shift_max
                optical = sheared(near_a, step_a, z, start, width, amount, weight, lane)
                glowing = sheared(near_e, step_e, z, start, width, amount, weight, lane)
                for i in range(many):
                    trans = jnp.exp(-optical[i])
                    cols = slice(i * lanes, (i + 1) * lanes)
                    keep[z, 0, :, cols] = trans
                    keep[z, 1, :, cols] = glowing[i]
                    keep[z, 2, :, cols] = run[i]
                    run[i] = run[i] * trans
            behind = entering(1)
            for z in reversed(range(slices)):
                for i in range(many):
                    cols = slice(i * lanes, (i + 1) * lanes)
                    trans, glow, before = keep[z, 0, :, cols], keep[z, 1, :, cols], keep[z, 2, :, cols]
                    opaque = 1.0 - trans
                    at = pl.ds(pl.multiple_of(start + i * lanes, lanes), lanes)
                    grad_e[v, z, :, at] = before * opaque
                    grad_a[v, z, :, at] = before * trans * (glow - behind[i])
                    behind[i] = glow * opaque + trans * behind[i]
            return 0

        lax.fori_loop(0, columns // width, chunk_loop, 0)
        for z in range(slices):
            grad_a[v, z, :, columns:] = grad_a[v, z, :, :lanes]
            grad_e[v, z, :, columns:] = grad_e[v, z, :, :lanes]
        return 0

    lax.fori_loop(0, views, view_loop, 0)

    row = lax.broadcasted_iota(jnp.int32, (rows, columns), 0)
    col = lax.broadcasted_iota(jnp.int32, (rows, columns), 1)

    def slice_loop(z, _):
        for f, (field_ref, grad, out, reg) in enumerate(
            ((absorb_ref, grad_a, ga_ref, reg_absorb), (emit_ref, grad_e, ge_ref, reg_emit))
        ):
            near, far = [], []
            for ch in range(columns // width):
                total_near, total_far = None, None
                for v in range(views):
                    weight = frac_ref[v]
                    parts = tiles(grad[v, z, :, ch * width : (ch + 1) * width + lanes])
                    moved = advance(parts, shift_max - offs_ref[v, z], lane)
                    a = [(1.0 - weight) * m for m in moved]
                    b = [weight * m for m in moved]
                    total_near = a if v == 0 else [x + y for x, y in zip(total_near, a)]
                    total_far = b if v == 0 else [x + y for x, y in zip(total_far, b)]
                near += total_near
                far += total_far
            total = pltpu.roll(jnp.concatenate(near, axis=1), shift_max, axis=1)
            total += pltpu.roll(jnp.concatenate(far, axis=1), shift_max + 1, axis=1)
            field = field_ref[z].astype(jnp.float32)
            edge = rim_ref[f, pl.ds(z, 1), :]
            up = jnp.where(row == 0, jnp.where(lower, 0.0, edge), pltpu.roll(field, 1, axis=0))
            down = jnp.where(
                row == rows - 1, jnp.where(lower, edge, 0.0), pltpu.roll(field, rows - 1, axis=0)
            )
            left = jnp.where(col == 0, 0.0, pltpu.roll(field, 1, axis=1))
            right = jnp.where(col == columns - 1, 0.0, pltpu.roll(field, columns - 1, axis=1))
            out[z] = total - reg * (down + up + right + left - 4.0 * field)
        return 0

    lax.fori_loop(0, slices, slice_loop, 0)


def body(absorb, emission, measured, camera_view, offsets, fractions):
    slices, rows, columns = absorb.shape
    views = offsets.shape[0]
    count = lax.axis_size("depth")
    piece = columns // count
    whole = pl.BlockSpec(memory_space=pltpu.VMEM)
    scalar = pl.BlockSpec(memory_space=pltpu.SMEM)
    f32 = jnp.float32
    wide = pltpu.VMEM((slices, rows, columns + lanes), f32)
    blocks = (count, views, 2, rows, piece)
    sums, edge = pl.pallas_call(
        first_kernel,
        out_shape=(
            jax.ShapeDtypeStruct(blocks, f32),
            jax.ShapeDtypeStruct((2, slices, columns), f32),
        ),
        in_specs=[whole, whole, scalar, scalar],
        out_specs=(whole, whole),
        scratch_shapes=[wide] * 4,
        compiler_params=vmem,
        name="bricks",
    )(absorb, emission, offsets, fractions)
    dma = pltpu.SemaphoreType.DMA
    back, rim = pl.pallas_call(
        cross_kernel,
        out_shape=(
            jax.ShapeDtypeStruct(blocks, f32),
            jax.ShapeDtypeStruct((2, slices, columns), f32),
        ),
        in_specs=[whole, whole, scalar, whole],
        out_specs=(whole, whole),
        scratch_shapes=[
            pltpu.VMEM(blocks, f32),
            pltpu.VMEM(blocks, f32),
            dma((views, count)), dma((views, count)), dma((views, count)), dma((views, count)),
            dma, dma,
        ],
        compiler_params=pltpu.CompilerParams(
            vmem_limit_bytes=32 * 1024 * 1024, collective_id=0, has_side_effects=True
        ),
        name="exchange",
    )(sums, measured, camera_view, edge)
    grads = pltpu.VMEM((views, slices, rows, columns + lanes), f32)
    return pl.pallas_call(
        second_kernel,
        out_shape=(
            jax.ShapeDtypeStruct(absorb.shape, f32),
            jax.ShapeDtypeStruct(absorb.shape, f32),
        ),
        in_specs=[whole, whole, scalar, scalar, whole, whole],
        out_specs=(whole, whole),
        scratch_shapes=[wide] * 4 + [grads, grads, pltpu.VMEM((slices, 3, rows, 512), f32)],
        compiler_params=vmem,
        name="gradients",
    )(absorb, emission, offsets, fractions, back, rim)


def solution(mesh):
    placed = (
        P("depth", ("groups", "lat"), None),
        P("depth", ("groups", "lat"), None),
        P(None, ("groups", "lat"), None),
        P(),
        P(None, "depth"),
        P(),
    )
    return jax.shard_map(
        body,
        mesh=mesh,
        in_specs=placed,
        out_specs=(P("depth", ("groups", "lat"), None), P("depth", ("groups", "lat"), None)),
        check_vma=False,
    )
```

```python
import functools

import jax
import jax.numpy as jnp
from jax import lax
from jax.experimental import pallas as pl
from jax.experimental.pallas import tpu as pltpu
from jax.sharding import PartitionSpec as P

reg_absorb = 20.0
reg_emit = 0.05
shift_max = 32
lanes = 128
vmem = pltpu.CompilerParams(vmem_limit_bytes=48 * 1024 * 1024)
MESH = pl.DeviceIdType.MESH


def tiles(value):
    return [value[:, i * lanes : (i + 1) * lanes] for i in range(value.shape[1] // lanes)]


def advance(parts, amount, lane):
    turned = [pltpu.roll(part, (lanes - amount) & (lanes - 1), axis=1) for part in parts]
    keep = lane < lanes - amount
    return [jnp.where(keep, turned[i], turned[i + 1]) for i in range(len(parts) - 1)]


def fill(field_ref, near_ref, step_ref, z):
    columns = field_ref.shape[2]
    field = field_ref[z].astype(jnp.float32)
    near = pltpu.roll(field, shift_max, axis=1)
    step = pltpu.roll(field, shift_max - 1, axis=1) - near
    near_ref[z, :, :columns] = near
    near_ref[z, :, columns:] = near[:, :lanes]
    step_ref[z, :, :columns] = step
    step_ref[z, :, columns:] = step[:, :lanes]


def sheared(near_ref, step_ref, z, start, width, amount, weight, lane):
    near = near_ref[z, :, pl.ds(start, width + lanes)]
    step = step_ref[z, :, pl.ds(start, width + lanes)]
    return advance(tiles(near + weight * step), amount, lane)


def first_kernel(
    absorb_ref, emit_ref, offs_ref, frac_ref, out_ref, edge_ref, near_a, step_a, near_e, step_e
):
    slices, rows, columns = absorb_ref.shape
    views = frac_ref.shape[0]
    piece = out_ref.shape[4]
    width = 1024
    lower = lax.axis_index("lat") == 0
    for z in range(slices):
        fill(absorb_ref, near_a, step_a, z)
        fill(emit_ref, near_e, step_e, z)
        for f, ref in enumerate((absorb_ref, emit_ref)):
            field = ref[z].astype(jnp.float32)
            edge_ref[f, z : z + 1, :] = jnp.where(lower, field[rows - 1 :], field[:1])
    lane = lax.broadcasted_iota(jnp.int32, (rows, lanes), 1)
    many = width // lanes

    def view_loop(v, _):
        weight = frac_ref[v]

        def chunk_loop(ch, _):
            start = pl.multiple_of(ch * width, width)
            run, light = None, None
            for z in range(slices):
                amount = offs_ref[v, z] + shift_max
                optical = sheared(near_a, step_a, z, start, width, amount, weight, lane)
                glowing = sheared(near_e, step_e, z, start, width, amount, weight, lane)
                trans = [jnp.exp(-o) for o in optical]
                radiance = [g * (1.0 - t) for g, t in zip(glowing, trans)]
                if z == 0:
                    run, light = trans, radiance
                else:
                    light = [l + r * x for l, r, x in zip(light, run, radiance)]
                    run = [r * t for r, t in zip(run, trans)]
            per = piece // lanes
            for i in range(many):
                dest = ch * (width // piece) + i // per
                cols = slice((i % per) * lanes, (i % per + 1) * lanes)
                out_ref[v, dest, 0, :, cols] = run[i]
                out_ref[v, dest, 1, :, cols] = light[i]
            return 0

        return lax.fori_loop(0, columns // width, chunk_loop, 0)

    lax.fori_loop(0, views, view_loop, 0)


def cross_kernel(
    mine_ref, measured_ref, cam_ref, edge_ref, back_ref, rim_ref,
    other, pair, got, sent, ret, give, sa, ra, sb, rb, sd, rd, sc, rc, s3, r3,
):
    views, count, _, rows, piece = mine_ref.shape
    cameras = measured_ref.shape[0]
    half = count // 2
    me = lax.axis_index("depth")
    lat = lax.axis_index("lat")
    high, low = me // 2, lax.rem(me, 2)
    partner = high * 2 + 1 - low
    near = low == 0
    barrier = pltpu.get_barrier_semaphore()

    def line(p):
        return lax.rem(high + p, half)

    def send(src, dst, send_sem, recv_sem, to):
        return pltpu.make_async_remote_copy(
            src_ref=src, dst_ref=dst, send_sem=send_sem, recv_sem=recv_sem,
            device_id={"depth": to}, device_id_type=MESH,
        )

    for p in range(1, half):
        pl.semaphore_signal(
            barrier, inc=1, device_id={"depth": line(p) * 2 + low}, device_id_type=MESH
        )
    pl.semaphore_signal(barrier, inc=1, device_id={"depth": partner}, device_id_type=MESH)
    pl.semaphore_signal(barrier, inc=1, device_id={"lat": 1 - lat}, device_id_type=MESH)
    pl.semaphore_wait(barrier, half + 1)

    def to_pair(v):
        src = mine_ref.at[v, pl.ds((1 - low) * half, half)]
        return send(src, other.at[v], sa.at[v], ra.at[v], partner)

    def to_line(v, p):
        to = line(p)
        return send(pair.at[v, to], got.at[v, high], sb.at[v, p], rb.at[v, p], to * 2 + low)

    def from_line(v, p):
        to = line(p)
        return send(sent.at[v, to], ret.at[v, high], sd.at[v, p], rd.at[v, p], to * 2 + low)

    def from_pair(v):
        dst = back_ref.at[v, pl.ds(low * half, half)]
        return send(give.at[v], dst, sc.at[v], rc.at[v], partner)

    for v in range(views):
        to_pair(v).start()
    rim = pltpu.make_async_remote_copy(
        src_ref=edge_ref, dst_ref=rim_ref, send_sem=s3, recv_sem=r3,
        device_id={"lat": 1 - lat}, device_id_type=MESH,
    )
    rim.start()
    start = pl.multiple_of((low * half + high) * piece, piece)

    def combine(v):
        to_pair(v).wait_recv()
        for p in [*range(1, half), 0]:
            h = line(p)
            own_t, own_l = mine_ref[v, low * half + h, 0], mine_ref[v, low * half + h, 1]
            oth_t, oth_l = other[v, h, 0], other[v, h, 1]
            trans = own_t * oth_t
            light = jnp.where(near, own_l + own_t * oth_l, oth_l + oth_t * own_l)
            if p:
                pair[v, h, 0] = trans
                pair[v, h, 1] = light
                to_line(v, p).start()
            else:
                got[v, h, 0] = trans
                got[v, h, 1] = light

    def scan(v):
        for p in range(1, half):
            to_line(v, p).wait_recv()
        fronts = [jnp.ones((rows, piece), jnp.float32)]
        for j in range(half - 1):
            fronts.append(fronts[-1] * got[v, j, 0])
        behind = jnp.zeros((rows, piece), jnp.float32)
        for j in reversed(range(half)):
            sent[v, j, 1] = behind
            behind = got[v, j, 1] + got[v, j, 0] * behind
        adjoint = jnp.zeros((rows, piece), jnp.float32)
        for k in range(cameras):
            seen = jnp.where(cam_ref[k, 0] == v, 1.0, 0.0).astype(jnp.float32)
            adjoint += seen * (behind - measured_ref[k, :, pl.ds(start, piece)])
        for j in range(half):
            sent[v, j, 0] = adjoint * fronts[j]
        for p in range(1, half):
            from_line(v, p).start()
        ret[v, high] = sent[v, high]

    def spread(v):
        for p in range(1, half):
            from_line(v, p).wait_recv()
        for h in range(half):
            at = low * half + h
            own_t, own_l = mine_ref[v, at, 0], mine_ref[v, at, 1]
            oth_t, oth_l = other[v, h, 0], other[v, h, 1]
            front, behind = ret[v, h, 0], ret[v, h, 1]
            give[v, h, 0] = jnp.where(near, front * own_t, front)
            give[v, h, 1] = jnp.where(near, behind, own_l + own_t * behind)
            back_ref[v, at, 0] = jnp.where(near, front, front * oth_t)
            back_ref[v, at, 1] = jnp.where(near, oth_l + oth_t * behind, behind)
        from_pair(v).start()

    for turn in range(views + 2):
        if turn < views:
            combine(turn)
        if 0 <= turn - 1 < views:
            scan(turn - 1)
        if 0 <= turn - 2 < views:
            spread(turn - 2)
    rim.wait()
    for v in range(views):
        to_pair(v).wait_send()
        for p in range(1, half):
            to_line(v, p).wait_send()
            from_line(v, p).wait_send()
        from_pair(v).wait()


def second_kernel(
    absorb_ref, emit_ref, offs_ref, frac_ref, back_ref, rim_ref, ga_ref, ge_ref,
    near_a, step_a, near_e, step_e, grad_a, grad_e, keep,
):
    slices, rows, columns = absorb_ref.shape
    views = frac_ref.shape[0]
    piece = back_ref.shape[4]
    width = min(512, columns)
    lower = lax.axis_index("lat") == 0
    for z in range(slices):
        fill(absorb_ref, near_a, step_a, z)
        fill(emit_ref, near_e, step_e, z)
    lane = lax.broadcasted_iota(jnp.int32, (rows, lanes), 1)
    many = width // lanes
    per = piece // lanes

    def view_loop(v, _):
        weight = frac_ref[v]

        def chunk_loop(ch, _):
            start = pl.multiple_of(ch * width, width)

            def entering(q):
                if piece >= width:
                    first = ch // (piece // width)
                    inner = pl.multiple_of((ch % (piece // width)) * width, width)
                    return tiles(back_ref[v, first, q, :, pl.ds(inner, width)])
                parts = []
                for i in range(many):
                    cols = slice((i % per) * lanes, (i % per + 1) * lanes)
                    parts.append(back_ref[v, ch * (width // piece) + i // per, q, :, cols])
                return parts

            run = entering(0)
            for z in range(slices):
                amount = offs_ref[v, z] + shift_max
                optical = sheared(near_a, step_a, z, start, width, amount, weight, lane)
                glowing = sheared(near_e, step_e, z, start, width, amount, weight, lane)
                for i in range(many):
                    trans = jnp.exp(-optical[i])
                    cols = slice(i * lanes, (i + 1) * lanes)
                    keep[z, 0, :, cols] = trans
                    keep[z, 1, :, cols] = glowing[i]
                    keep[z, 2, :, cols] = run[i]
                    run[i] = run[i] * trans
            behind = entering(1)
            for z in reversed(range(slices)):
                for i in range(many):
                    cols = slice(i * lanes, (i + 1) * lanes)
                    trans, glow, before = keep[z, 0, :, cols], keep[z, 1, :, cols], keep[z, 2, :, cols]
                    opaque = 1.0 - trans
                    at = pl.ds(pl.multiple_of(start + i * lanes, lanes), lanes)
                    grad_e[v, z, :, at] = before * opaque
                    grad_a[v, z, :, at] = before * trans * (glow - behind[i])
                    behind[i] = glow * opaque + trans * behind[i]
            return 0

        lax.fori_loop(0, columns // width, chunk_loop, 0)
        for z in range(slices):
            grad_a[v, z, :, columns:] = grad_a[v, z, :, :lanes]
            grad_e[v, z, :, columns:] = grad_e[v, z, :, :lanes]
        return 0

    lax.fori_loop(0, views, view_loop, 0)

    row = lax.broadcasted_iota(jnp.int32, (rows, columns), 0)
    col = lax.broadcasted_iota(jnp.int32, (rows, columns), 1)

    def slice_loop(z, _):
        for f, (field_ref, grad, out, reg) in enumerate(
            ((absorb_ref, grad_a, ga_ref, reg_absorb), (emit_ref, grad_e, ge_ref, reg_emit))
        ):
            near, far = [], []
            for ch in range(columns // width):
                total_near, total_far = None, None
                for v in range(views):
                    weight = frac_ref[v]
                    parts = tiles(grad[v, z, :, ch * width : (ch + 1) * width + lanes])
                    moved = advance(parts, shift_max - offs_ref[v, z], lane)
                    a = [(1.0 - weight) * m for m in moved]
                    b = [weight * m for m in moved]
                    total_near = a if v == 0 else [x + y for x, y in zip(total_near, a)]
                    total_far = b if v == 0 else [x + y for x, y in zip(total_far, b)]
                near += total_near
                far += total_far
            total = pltpu.roll(jnp.concatenate(near, axis=1), shift_max, axis=1)
            total += pltpu.roll(jnp.concatenate(far, axis=1), shift_max + 1, axis=1)
            field = field_ref[z].astype(jnp.float32)
            edge = rim_ref[f, pl.ds(z, 1), :]
            up = jnp.where(row == 0, jnp.where(lower, 0.0, edge), pltpu.roll(field, 1, axis=0))
            down = jnp.where(
                row == rows - 1, jnp.where(lower, edge, 0.0), pltpu.roll(field, rows - 1, axis=0)
            )
            left = jnp.where(col == 0, 0.0, pltpu.roll(field, 1, axis=1))
            right = jnp.where(col == columns - 1, 0.0, pltpu.roll(field, columns - 1, axis=1))
            out[z] = total - reg * (down + up + right + left - 4.0 * field)
        return 0

    lax.fori_loop(0, slices, slice_loop, 0)


def body(absorb, emission, measured, camera_view, offsets, fractions):
    slices, rows, columns = absorb.shape
    views = offsets.shape[0]
    count = lax.axis_size("depth")
    piece = columns // count
    whole = pl.BlockSpec(memory_space=pltpu.VMEM)
    scalar = pl.BlockSpec(memory_space=pltpu.SMEM)
    f32 = jnp.float32
    wide = pltpu.VMEM((slices, rows, columns + lanes), f32)
    blocks = (views, count, 2, rows, piece)
    half = count // 2
    part = pltpu.VMEM((views, half, 2, rows, piece), f32)
    sums, edge = pl.pallas_call(
        first_kernel,
        out_shape=(
            jax.ShapeDtypeStruct(blocks, f32),
            jax.ShapeDtypeStruct((2, slices, columns), f32),
        ),
        in_specs=[whole, whole, scalar, scalar],
        out_specs=(whole, whole),
        scratch_shapes=[wide] * 4,
        compiler_params=vmem,
        name="bricks",
    )(absorb, emission, offsets, fractions)
    dma = pltpu.SemaphoreType.DMA
    back, rim = pl.pallas_call(
        cross_kernel,
        out_shape=(
            jax.ShapeDtypeStruct(blocks, f32),
            jax.ShapeDtypeStruct((2, slices, columns), f32),
        ),
        in_specs=[whole, whole, scalar, whole],
        out_specs=(whole, whole),
        scratch_shapes=[
            *[part] * 6,
            *[dma((views,))] * 2, *[dma((views, half))] * 4, *[dma((views,))] * 2,
            dma, dma,
        ],
        compiler_params=pltpu.CompilerParams(
            vmem_limit_bytes=32 * 1024 * 1024, collective_id=0, has_side_effects=True
        ),
        name="exchange",
    )(sums, measured, camera_view, edge)
    grads = pltpu.VMEM((views, slices, rows, columns + lanes), f32)
    return pl.pallas_call(
        second_kernel,
        out_shape=(
            jax.ShapeDtypeStruct(absorb.shape, f32),
            jax.ShapeDtypeStruct(absorb.shape, f32),
        ),
        in_specs=[whole, whole, scalar, scalar, whole, whole],
        out_specs=(whole, whole),
        scratch_shapes=[wide] * 4 + [grads, grads, pltpu.VMEM((slices, 3, rows, 512), f32)],
        compiler_params=vmem,
        name="gradients",
    )(absorb, emission, offsets, fractions, back, rim)


def solution(mesh):
    placed = (
        P("depth", ("groups", "lat"), None),
        P("depth", ("groups", "lat"), None),
        P(None, ("groups", "lat"), None),
        P(),
        P(None, "depth"),
        P(),
    )
    return jax.shard_map(
        body,
        mesh=mesh,
        in_specs=placed,
        out_specs=(P("depth", ("groups", "lat"), None), P("depth", ("groups", "lat"), None)),
        check_vma=False,
    )
```

```python
import jax
import jax.numpy as jnp
from jax import lax
from jax.experimental import pallas as pl
from jax.experimental.pallas import tpu as pltpu
from jax.sharding import PartitionSpec as P

reg_absorb = 20.0
reg_emit = 0.05
shift_max = 32
lanes = 128
MESH = pl.DeviceIdType.MESH


def tiles(value):
    return [value[:, i * lanes : (i + 1) * lanes] for i in range(value.shape[1] // lanes)]


def advance(parts, amount, lane):
    turned = [pltpu.roll(part, (lanes - amount) & (lanes - 1), axis=1) for part in parts]
    keep = lane < lanes - amount
    return [jnp.where(keep, turned[i], turned[i + 1]) for i in range(len(parts) - 1)]


def fill(field_ref, near_ref, step_ref, z):
    columns = field_ref.shape[2]
    field = field_ref[z].astype(jnp.float32)
    near = pltpu.roll(field, shift_max, axis=1)
    step = pltpu.roll(field, shift_max - 1, axis=1) - near
    near_ref[z, :, :columns] = near
    near_ref[z, :, columns:] = near[:, :lanes]
    step_ref[z, :, :columns] = step
    step_ref[z, :, columns:] = step[:, :lanes]


def sheared(near_ref, step_ref, z, start, width, amount, weight, lane):
    near = near_ref[z, :, pl.ds(start, width + lanes)]
    step = step_ref[z, :, pl.ds(start, width + lanes)]
    return advance(tiles(near + weight * step), amount, lane)


def fused_kernel(
    absorb_ref, emit_ref, measured_ref, cam_ref, offs_ref, frac_ref, ga_ref, ge_ref,
    near_a, step_a, near_e, step_e, seen_ref, edge_ref, rim_ref, mine_ref, back_ref,
    other, pair, got, sent, ret, give, keep, grad_a, grad_e, sum_a, sum_e,
    sa, ra, sb, rb, sd, rd, sc, rc, s3, r3, sm,
):
    slices, rows, columns = absorb_ref.shape
    views, count, _, _, piece = mine_ref.shape
    cameras = measured_ref.shape[0]
    half = count // 2
    me = lax.axis_index("depth")
    lat = lax.axis_index("lat")
    high, low = me // 2, lax.rem(me, 2)
    partner = high * 2 + 1 - low
    near = low == 0
    barrier = pltpu.get_barrier_semaphore()

    def line(p):
        return lax.rem(high + p, half)

    def send(src, dst, send_sem, recv_sem, to):
        return pltpu.make_async_remote_copy(
            src_ref=src, dst_ref=dst, send_sem=send_sem, recv_sem=recv_sem,
            device_id={"depth": to}, device_id_type=MESH,
        )

    for p in range(1, half):
        pl.semaphore_signal(
            barrier, inc=1, device_id={"depth": line(p) * 2 + low}, device_id_type=MESH
        )
    pl.semaphore_signal(barrier, inc=1, device_id={"depth": partner}, device_id_type=MESH)
    pl.semaphore_signal(barrier, inc=1, device_id={"lat": 1 - lat}, device_id_type=MESH)
    def to_pair(v):
        src = mine_ref.at[v, pl.ds((1 - low) * half, half)]
        return send(src, other.at[v], sa.at[v], ra.at[v], partner)

    def to_line(v, p):
        to = line(p)
        return send(pair.at[v, to], got.at[v, high], sb.at[v, p], rb.at[v, p], to * 2 + low)

    def from_line(v, p):
        to = line(p)
        return send(sent.at[v, to], ret.at[v, high], sd.at[v, p], rd.at[v, p], to * 2 + low)

    def from_pair(v):
        dst = back_ref.at[v, pl.ds(low * half, half)]
        return send(give.at[v], dst, sc.at[v], rc.at[v], partner)

    start = pl.multiple_of((low * half + high) * piece, piece)
    images = pltpu.make_async_copy(measured_ref.at[:, :, pl.ds(start, piece)], seen_ref, sm)
    images.start()
    lower = lat == 0
    for z in range(slices):
        fill(absorb_ref, near_a, step_a, z)
        fill(emit_ref, near_e, step_e, z)
        for f, ref in enumerate((absorb_ref, emit_ref)):
            field = ref[z].astype(jnp.float32)
            edge_ref[f, z : z + 1, :] = jnp.where(lower, field[rows - 1 :], field[:1])
    pl.semaphore_wait(barrier, half + 1)
    rim = pltpu.make_async_remote_copy(
        src_ref=edge_ref, dst_ref=rim_ref, send_sem=s3, recv_sem=r3,
        device_id={"lat": 1 - lat}, device_id_type=MESH,
    )
    rim.start()

    def combine(v):
        to_pair(v).wait_recv()
        for p in [*range(1, half), 0]:
            h = line(p)
            own_t, own_l = mine_ref[v, low * half + h, 0], mine_ref[v, low * half + h, 1]
            oth_t, oth_l = other[v, h, 0], other[v, h, 1]
            trans = own_t * oth_t
            light = jnp.where(near, own_l + own_t * oth_l, oth_l + oth_t * own_l)
            if p:
                pair[v, h, 0] = trans
                pair[v, h, 1] = light
                to_line(v, p).start()
            else:
                got[v, h, 0] = trans
                got[v, h, 1] = light

    def scan(v):
        for p in range(1, half):
            to_line(v, p).wait_recv()
        fronts = [jnp.ones((rows, piece), jnp.float32)]
        for j in range(half - 1):
            fronts.append(fronts[-1] * got[v, j, 0])
        behind = jnp.zeros((rows, piece), jnp.float32)
        for j in reversed(range(half)):
            sent[v, j, 1] = behind
            behind = got[v, j, 1] + got[v, j, 0] * behind
        adjoint = jnp.zeros((rows, piece), jnp.float32)
        for k in range(cameras):
            seen = jnp.where(cam_ref[k : k + 1, :] == v, 1.0, 0.0).astype(jnp.float32)
            adjoint += seen * (behind - seen_ref[k])
        for j in range(half):
            sent[v, j, 0] = adjoint * fronts[j]
        for p in range(1, half):
            from_line(v, p).start()
        ret[v, high] = sent[v, high]

    def spread(v):
        for p in range(1, half):
            from_line(v, p).wait_recv()
        for h in range(half):
            at = low * half + h
            own_t, own_l = mine_ref[v, at, 0], mine_ref[v, at, 1]
            oth_t, oth_l = other[v, h, 0], other[v, h, 1]
            front, behind = ret[v, h, 0], ret[v, h, 1]
            give[v, h, 0] = jnp.where(near, front * own_t, front)
            give[v, h, 1] = jnp.where(near, behind, own_l + own_t * behind)
            back_ref[v, at, 0] = jnp.where(near, front, front * oth_t)
            back_ref[v, at, 1] = jnp.where(near, oth_l + oth_t * behind, behind)
        from_pair(v).start()

    lane = lax.broadcasted_iota(jnp.int32, (rows, lanes), 1)
    per = piece // lanes
    wide = 1024

    def forward(v):
        weight = frac_ref[v]

        def chunk_loop(ch, _):
            begin = pl.multiple_of(ch * wide, wide)
            run, light = None, None
            for z in range(slices):
                amount = offs_ref[v, z] + shift_max
                optical = sheared(near_a, step_a, z, begin, wide, amount, weight, lane)
                glowing = sheared(near_e, step_e, z, begin, wide, amount, weight, lane)
                trans = [jnp.exp(-o) for o in optical]
                radiance = [g * (1.0 - t) for g, t in zip(glowing, trans)]
                at = pl.ds(begin, wide)
                keep[v, z, 0, :, at] = jnp.concatenate(trans, axis=1)
                keep[v, z, 1, :, at] = jnp.concatenate(glowing, axis=1)
                if z == 0:
                    run, light = trans, radiance
                else:
                    keep[v, z, 2, :, at] = jnp.concatenate(run, axis=1)
                    light = [l + r * x for l, r, x in zip(light, run, radiance)]
                    run = [r * t for r, t in zip(run, trans)]
            for i in range(wide // lanes):
                dest = ch * (wide // piece) + i // per
                cols = slice((i % per) * lanes, (i % per + 1) * lanes)
                mine_ref[v, dest, 0, :, cols] = run[i]
                mine_ref[v, dest, 1, :, cols] = light[i]
            return 0

        lax.fori_loop(0, columns // wide, chunk_loop, 0)
        to_pair(v).start()

    def gradient(v, side):
        def piece_loop(h, _):
            p = side * half + h
            at = pl.ds(pl.multiple_of(p * piece, piece), piece)
            front, behind = back_ref[v, p, 0], back_ref[v, p, 1]
            for z in reversed(range(slices)):
                trans, glow = keep[v, z, 0, :, at], keep[v, z, 1, :, at]
                before = front * keep[v, z, 2, :, at] if z else front
                opaque = 1.0 - trans
                grad_e[z, :, at] = before * opaque
                grad_a[z, :, at] = before * trans * (glow - behind)
                behind = glow * opaque + trans * behind
            return 0

        lax.fori_loop(0, half, piece_loop, 0)

    def finish(v):
        from_pair(v).wait_recv()
        gradient(v, 1 - low)
        weight = frac_ref[v]
        for grad in (grad_a, grad_e):
            for z in range(slices):
                grad[z, :, columns:] = grad[z, :, :lanes]

        def slice_loop(z, _):
            amount = shift_max - offs_ref[v, z]
            for grad, total, out in ((grad_a, sum_a, ga_ref), (grad_e, sum_e, ge_ref)):
                near, far = [], []
                for ch in range(columns // wide):
                    parts = tiles(grad[z, :, ch * wide : (ch + 1) * wide + lanes])
                    moved = jnp.concatenate(advance(parts, amount, lane), axis=1)
                    at = slice(ch * wide, (ch + 1) * wide)
                    a, b = (1.0 - weight) * moved, weight * moved
                    if v:
                        a, b = a + total[0, z, :, at], b + total[1, z, :, at]
                    if v < views - 1:
                        total[0, z, :, at] = a
                        total[1, z, :, at] = b
                    near.append(a)
                    far.append(b)
                if v == views - 1:
                    far = pltpu.roll(jnp.concatenate(far, axis=1), 1, axis=1)
                    both = jnp.concatenate(near, axis=1) + far
                    out[z] = out[z] + pltpu.roll(both, shift_max, axis=1)
            return 0

        lax.fori_loop(0, slices, slice_loop, 0)

    def smooth(f, field_ref, out, reg):
        row = lax.broadcasted_iota(jnp.int32, (rows, columns), 0)
        col = lax.broadcasted_iota(jnp.int32, (rows, columns), 1)
        for z in range(slices):
            field = field_ref[z].astype(jnp.float32)
            edge = rim_ref[f, z : z + 1, :]
            up = jnp.where(row == 0, jnp.where(lower, 0.0, edge), pltpu.roll(field, 1, axis=0))
            down = jnp.where(
                row == rows - 1, jnp.where(lower, edge, 0.0), pltpu.roll(field, rows - 1, axis=0)
            )
            left = jnp.where(col == 0, 0.0, pltpu.roll(field, 1, axis=1))
            right = jnp.where(col == columns - 1, 0.0, pltpu.roll(field, columns - 1, axis=1))
            out[z] = -reg * (down + up + right + left - 4.0 * field)

    for v in range(views - 1):
        forward(v)
    images.wait()
    for turn in range(views + 3):
        if turn < views:
            combine(turn)
        if turn == 0:
            forward(views - 1)
        if 0 <= turn - 1 < views:
            scan(turn - 1)
        if turn == 1:
            rim.wait_recv()
            smooth(0, absorb_ref, ga_ref, reg_absorb)
            smooth(1, emit_ref, ge_ref, reg_emit)
        if 0 <= turn - 2 < views:
            spread(turn - 2)
        if 0 <= turn - 3 < views:
            finish(turn - 3)
        if 0 <= turn - 2 < views:
            gradient(turn - 2, low)
    rim.wait_send()
    for v in range(views):
        to_pair(v).wait_send()
        for p in range(1, half):
            to_line(v, p).wait_send()
            from_line(v, p).wait_send()
        from_pair(v).wait_send()


def body(absorb, emission, measured, camera_view, offsets, fractions):
    slices, rows, columns = absorb.shape
    views, cameras = offsets.shape[0], measured.shape[0]
    count = lax.axis_size("depth")
    half, piece = count // 2, columns // count
    whole = pl.BlockSpec(memory_space=pltpu.VMEM)
    scalar = pl.BlockSpec(memory_space=pltpu.SMEM)
    dma = pltpu.SemaphoreType.DMA

    def room(*shape):
        return pltpu.VMEM(shape, jnp.float32)

    padded = room(slices, rows, columns + lanes)
    return pl.pallas_call(
        fused_kernel,
        out_shape=(
            jax.ShapeDtypeStruct(absorb.shape, jnp.float32),
            jax.ShapeDtypeStruct(absorb.shape, jnp.float32),
        ),
        in_specs=[whole, whole, pl.BlockSpec(memory_space=pl.ANY), whole, scalar, scalar],
        out_specs=(whole, whole),
        scratch_shapes=[
            *[padded] * 4,
            room(cameras, rows, piece),
            *[room(2, slices, columns)] * 2,
            *[room(views, count, 2, rows, piece)] * 2,
            *[room(views, half, 2, rows, piece)] * 6,
            room(views, slices, 3, rows, columns),
            *[padded] * 2,
            *[room(2, slices, rows, columns)] * 2,
            *[dma((views,))] * 2, *[dma((views, half))] * 4, *[dma((views,))] * 2,
            dma, dma, dma,
        ],
        compiler_params=pltpu.CompilerParams(
            vmem_limit_bytes=52 * 1024 * 1024, collective_id=0, has_side_effects=True
        ),
        name="tomography",
    )(absorb, emission, measured, camera_view, offsets, fractions)


def solution(mesh):
    placed = (
        P("depth", ("groups", "lat"), None),
        P("depth", ("groups", "lat"), None),
        P(None, ("groups", "lat"), None),
        P(),
        P(None, "depth"),
        P(),
    )
    return jax.shard_map(
        body,
        mesh=mesh,
        in_specs=placed,
        out_specs=(P("depth", ("groups", "lat"), None), P("depth", ("groups", "lat"), None)),
        check_vma=False,
    )
```

```python
import jax
import jax.numpy as jnp
from jax import lax
from jax.experimental import pallas as pl
from jax.experimental.pallas import tpu as pltpu
from jax.sharding import PartitionSpec as P

reg_absorb = 20.0
reg_emit = 0.05
shift_max = 32
lanes = 128
MESH = pl.DeviceIdType.MESH


def tiles(value):
    return [value[:, i * lanes : (i + 1) * lanes] for i in range(value.shape[1] // lanes)]


def advance(parts, amount, lane):
    turned = [pltpu.roll(part, (lanes - amount) & (lanes - 1), axis=1) for part in parts]
    keep = lane < lanes - amount
    return [jnp.where(keep, turned[i], turned[i + 1]) for i in range(len(parts) - 1)]


def fill(field_ref, near_ref, step_ref, z):
    columns = field_ref.shape[2]
    field = field_ref[z].astype(jnp.float32)
    near = pltpu.roll(field, shift_max, axis=1)
    step = pltpu.roll(field, shift_max - 1, axis=1) - near
    near_ref[z, :, :columns] = near
    near_ref[z, :, columns:] = near[:, :lanes]
    step_ref[z, :, :columns] = step
    step_ref[z, :, columns:] = step[:, :lanes]


def sheared(near_ref, step_ref, z, start, width, amount, weight, lane):
    near = near_ref[z, :, pl.ds(start, width + lanes)]
    step = step_ref[z, :, pl.ds(start, width + lanes)]
    return advance(tiles(near + weight * step), amount, lane)


def fused_kernel(
    absorb_hbm, emit_hbm, measured_ref, cam_ref, offs_ref, frac_ref, ga_ref, ge_ref,
    absorb_ref, emit_ref,
    near_a, step_a, near_e, step_e, seen_ref, edge_ref, rim_ref, mine_ref, back_ref,
    other, pair, got, sent, ret, give, keep, grad_a, grad_e, sum_a, sum_e,
    sa, ra, sb, rb, sd, rd, sc, rc, s3, r3, sm, si,
):
    slices, rows, columns = absorb_ref.shape
    views, count, _, _, piece = mine_ref.shape
    loads = [
        pltpu.make_async_copy(src, dst, si.at[i])
        for i, (src, dst) in enumerate(((absorb_hbm, absorb_ref), (emit_hbm, emit_ref)))
    ]
    for load in loads:
        load.start()
    cameras = measured_ref.shape[0]
    half = count // 2
    me = lax.axis_index("depth")
    lat = lax.axis_index("lat")
    high, low = me // 2, lax.rem(me, 2)
    partner = high * 2 + 1 - low
    near = low == 0
    barrier = pltpu.get_barrier_semaphore()

    def line(p):
        return lax.rem(high + p, half)

    def send(src, dst, send_sem, recv_sem, to):
        return pltpu.make_async_remote_copy(
            src_ref=src, dst_ref=dst, send_sem=send_sem, recv_sem=recv_sem,
            device_id={"depth": to}, device_id_type=MESH,
        )

    for p in range(1, half):
        pl.semaphore_signal(
            barrier, inc=1, device_id={"depth": line(p) * 2 + low}, device_id_type=MESH
        )
    pl.semaphore_signal(barrier, inc=1, device_id={"depth": partner}, device_id_type=MESH)
    pl.semaphore_signal(barrier, inc=1, device_id={"lat": 1 - lat}, device_id_type=MESH)
    def to_pair(v):
        src = mine_ref.at[v, pl.ds((1 - low) * half, half)]
        return send(src, other.at[v], sa.at[v], ra.at[v], partner)

    def to_line(v, p):
        to = line(p)
        return send(pair.at[v, to], got.at[v, high], sb.at[v, p], rb.at[v, p], to * 2 + low)

    def from_line(v, p):
        to = line(p)
        return send(sent.at[v, to], ret.at[v, high], sd.at[v, p], rd.at[v, p], to * 2 + low)

    def from_pair(v):
        dst = back_ref.at[v, pl.ds(low * half, half)]
        return send(give.at[v], dst, sc.at[v], rc.at[v], partner)

    start = pl.multiple_of((low * half + high) * piece, piece)
    images = pltpu.make_async_copy(measured_ref.at[:, :, pl.ds(start, piece)], seen_ref, sm)
    images.start()
    lower = lat == 0
    for load in loads:
        load.wait()
    for z in range(slices):
        fill(absorb_ref, near_a, step_a, z)
        fill(emit_ref, near_e, step_e, z)
        for f, ref in enumerate((absorb_ref, emit_ref)):
            field = ref[z].astype(jnp.float32)
            edge_ref[f, z : z + 1, :] = jnp.where(lower, field[rows - 1 :], field[:1])
    pl.semaphore_wait(barrier, half + 1)
    rim = pltpu.make_async_remote_copy(
        src_ref=edge_ref, dst_ref=rim_ref, send_sem=s3, recv_sem=r3,
        device_id={"lat": 1 - lat}, device_id_type=MESH,
    )
    rim.start()

    def combine(v):
        to_pair(v).wait_recv()
        if v + ahead < views - 1:
            to_pair(v + ahead).start()
        for p in [*range(1, half), 0]:
            h = line(p)
            own_t, own_l = mine_ref[v, low * half + h, 0], mine_ref[v, low * half + h, 1]
            oth_t, oth_l = other[v, h, 0], other[v, h, 1]
            trans = own_t * oth_t
            light = jnp.where(near, own_l + own_t * oth_l, oth_l + oth_t * own_l)
            if p:
                pair[v, h, 0] = trans
                pair[v, h, 1] = light
                to_line(v, p).start()
            else:
                got[v, h, 0] = trans
                got[v, h, 1] = light

    def scan(v):
        for p in range(1, half):
            to_line(v, p).wait_recv()
        fronts = [jnp.ones((rows, piece), jnp.float32)]
        for j in range(half - 1):
            fronts.append(fronts[-1] * got[v, j, 0])
        behind = jnp.zeros((rows, piece), jnp.float32)
        for j in reversed(range(half)):
            sent[v, j, 1] = behind
            behind = got[v, j, 1] + got[v, j, 0] * behind
        adjoint = jnp.zeros((rows, piece), jnp.float32)
        for k in range(cameras):
            seen = jnp.where(cam_ref[0, k] == v, 1.0, 0.0).astype(jnp.float32)
            adjoint += seen * (behind - seen_ref[k])
        for j in range(half):
            sent[v, j, 0] = adjoint * fronts[j]
        for p in range(1, half):
            from_line(v, p).start()
        ret[v, high] = sent[v, high]

    def spread(v):
        for p in range(1, half):
            from_line(v, p).wait_recv()
        for h in range(half):
            at = low * half + h
            own_t, own_l = mine_ref[v, at, 0], mine_ref[v, at, 1]
            oth_t, oth_l = other[v, h, 0], other[v, h, 1]
            front, behind = ret[v, h, 0], ret[v, h, 1]
            give[v, h, 0] = jnp.where(near, front * own_t, front)
            give[v, h, 1] = jnp.where(near, behind, own_l + own_t * behind)
            back_ref[v, at, 0] = jnp.where(near, front, front * oth_t)
            back_ref[v, at, 1] = jnp.where(near, oth_l + oth_t * behind, behind)
        from_pair(v).start()

    lane = lax.broadcasted_iota(jnp.int32, (rows, lanes), 1)
    per = piece // lanes
    wide = 1024

    def forward(v):
        weight = frac_ref[v]

        def chunk_loop(ch, _):
            begin = pl.multiple_of(ch * wide, wide)
            run, light = None, None
            for z in range(slices):
                amount = offs_ref[v, z] + shift_max
                optical = sheared(near_a, step_a, z, begin, wide, amount, weight, lane)
                glowing = sheared(near_e, step_e, z, begin, wide, amount, weight, lane)
                trans = [jnp.exp(-o) for o in optical]
                radiance = [g * (1.0 - t) for g, t in zip(glowing, trans)]
                at = pl.ds(begin, wide)
                keep[v, z, 0, :, at] = jnp.concatenate(trans, axis=1)
                keep[v, z, 1, :, at] = jnp.concatenate(glowing, axis=1)
                if z == 0:
                    run, light = trans, radiance
                else:
                    keep[v, z, 2, :, at] = jnp.concatenate(run, axis=1)
                    light = [l + r * x for l, r, x in zip(light, run, radiance)]
                    run = [r * t for r, t in zip(run, trans)]
            for i in range(wide // lanes):
                dest = ch * (wide // piece) + i // per
                cols = slice((i % per) * lanes, (i % per + 1) * lanes)
                mine_ref[v, dest, 0, :, cols] = run[i]
                mine_ref[v, dest, 1, :, cols] = light[i]
            return 0

        lax.fori_loop(0, columns // wide, chunk_loop, 0)

    def gradient(v, side):
        def piece_loop(h, _):
            p = side * half + h
            at = pl.ds(pl.multiple_of(p * piece, piece), piece)
            front, behind = back_ref[v, p, 0], back_ref[v, p, 1]
            for z in reversed(range(slices)):
                trans, glow = keep[v, z, 0, :, at], keep[v, z, 1, :, at]
                before = front * keep[v, z, 2, :, at] if z else front
                opaque = 1.0 - trans
                grad_e[z, :, at] = before * opaque
                grad_a[z, :, at] = before * trans * (glow - behind)
                behind = glow * opaque + trans * behind
            return 0

        lax.fori_loop(0, half, piece_loop, 0)

    def finish(v):
        from_pair(v).wait_recv()
        gradient(v, 1 - low)
        weight = frac_ref[v]
        for grad in (grad_a, grad_e):
            for z in range(slices):
                grad[z, :, columns:] = grad[z, :, :lanes]

        def slice_loop(z, _):
            amount = shift_max - offs_ref[v, z]
            for grad, total, out in ((grad_a, sum_a, ga_ref), (grad_e, sum_e, ge_ref)):
                near, far = [], []
                for ch in range(columns // wide):
                    parts = tiles(grad[z, :, ch * wide : (ch + 1) * wide + lanes])
                    moved = jnp.concatenate(advance(parts, amount, lane), axis=1)
                    at = slice(ch * wide, (ch + 1) * wide)
                    a, b = (1.0 - weight) * moved, weight * moved
                    if v:
                        a, b = a + total[0, z, :, at], b + total[1, z, :, at]
                    if v < views - 1:
                        total[0, z, :, at] = a
                        total[1, z, :, at] = b
                    near.append(a)
                    far.append(b)
                if v == views - 1:
                    far = pltpu.roll(jnp.concatenate(far, axis=1), 1, axis=1)
                    both = jnp.concatenate(near, axis=1) + far
                    out[z] = out[z] + pltpu.roll(both, shift_max, axis=1)
            return 0

        lax.fori_loop(0, slices, slice_loop, 0)

    def smooth(f, field_ref, out, reg):
        row = lax.broadcasted_iota(jnp.int32, (rows, columns), 0)
        col = lax.broadcasted_iota(jnp.int32, (rows, columns), 1)
        for z in range(slices):
            field = field_ref[z].astype(jnp.float32)
            edge = rim_ref[f, z : z + 1, :]
            up = jnp.where(row == 0, jnp.where(lower, 0.0, edge), pltpu.roll(field, 1, axis=0))
            down = jnp.where(
                row == rows - 1, jnp.where(lower, edge, 0.0), pltpu.roll(field, rows - 1, axis=0)
            )
            left = jnp.where(col == 0, 0.0, pltpu.roll(field, 1, axis=1))
            right = jnp.where(col == columns - 1, 0.0, pltpu.roll(field, columns - 1, axis=1))
            out[z] = -reg * (down + up + right + left - 4.0 * field)

    ahead = 2
    for v in range(views - 1):
        forward(v)
        if v < ahead:
            to_pair(v).start()
    images.wait()
    for turn in range(views + 3):
        if turn < views:
            combine(turn)
        if turn == 0:
            forward(views - 1)
        if turn == views - 1 - ahead:
            to_pair(views - 1).start()
        if 0 <= turn - 1 < views:
            scan(turn - 1)
        if turn == 1:
            rim.wait_recv()
            smooth(0, absorb_ref, ga_ref, reg_absorb)
        if 0 <= turn - 2 < views:
            spread(turn - 2)
        if 0 <= turn - 3 < views:
            finish(turn - 3)
        if 0 <= turn - 2 < views:
            gradient(turn - 2, low)
        if turn == 2:
            smooth(1, emit_ref, ge_ref, reg_emit)
    rim.wait_send()
    for v in range(views):
        to_pair(v).wait_send()
        for p in range(1, half):
            to_line(v, p).wait_send()
            from_line(v, p).wait_send()
        from_pair(v).wait_send()


def body(absorb, emission, measured, camera_view, offsets, fractions):
    slices, rows, columns = absorb.shape
    views, cameras = offsets.shape[0], measured.shape[0]
    count = lax.axis_size("depth")
    half, piece = count // 2, columns // count
    whole = pl.BlockSpec(memory_space=pltpu.VMEM)
    hbm = pl.BlockSpec(memory_space=pltpu.HBM)
    scalar = pl.BlockSpec(memory_space=pltpu.SMEM)
    dma = pltpu.SemaphoreType.DMA

    def room(*shape):
        return pltpu.VMEM(shape, jnp.float32)

    padded = room(slices, rows, columns + lanes)
    return pl.pallas_call(
        fused_kernel,
        out_shape=(
            jax.ShapeDtypeStruct(absorb.shape, jnp.float32),
            jax.ShapeDtypeStruct(absorb.shape, jnp.float32),
        ),
        in_specs=[hbm, hbm, hbm, scalar, scalar, scalar],
        out_specs=(whole, whole),
        scratch_shapes=[
            *[pltpu.VMEM(absorb.shape, absorb.dtype)] * 2,
            *[padded] * 4,
            room(cameras, rows, piece),
            *[room(2, slices, columns)] * 2,
            *[room(views, count, 2, rows, piece)] * 2,
            *[room(views, half, 2, rows, piece)] * 6,
            room(views, slices, 3, rows, columns),
            *[padded] * 2,
            *[room(2, slices, rows, columns)] * 2,
            *[dma((views,))] * 2, *[dma((views, half))] * 4, *[dma((views,))] * 2,
            dma, dma, dma, dma((2,)),
        ],
        compiler_params=pltpu.CompilerParams(
            vmem_limit_bytes=60 * 1024 * 1024, collective_id=0, has_side_effects=True
        ),
        name="tomography",
    )(absorb, emission, measured, camera_view.T, offsets, fractions)


def solution(mesh):
    placed = (
        P("depth", ("groups", "lat"), None),
        P("depth", ("groups", "lat"), None),
        P(None, ("groups", "lat"), None),
        P(),
        P(None, "depth"),
        P(),
    )
    return jax.shard_map(
        body,
        mesh=mesh,
        in_specs=placed,
        out_specs=(P("depth", ("groups", "lat"), None), P("depth", ("groups", "lat"), None)),
        check_vma=False,
    )
```

```python
import jax
import jax.numpy as jnp
from jax import lax
from jax.experimental import pallas as pl
from jax.experimental.pallas import tpu as pltpu
from jax.sharding import PartitionSpec as P

reg_absorb = 20.0
reg_emit = 0.05
shift_max = 32
lanes = 128
MESH = pl.DeviceIdType.MESH


def tiles(value):
    return [value[:, i * lanes : (i + 1) * lanes] for i in range(value.shape[1] // lanes)]


def advance(parts, amount, lane):
    turned = [pltpu.roll(part, (lanes - amount) & (lanes - 1), axis=1) for part in parts]
    keep = lane < lanes - amount
    return [jnp.where(keep, turned[i], turned[i + 1]) for i in range(len(parts) - 1)]


def fill(field_ref, near_ref, step_ref, z):
    columns = field_ref.shape[2]
    field = field_ref[z].astype(jnp.float32)
    near = pltpu.roll(field, shift_max, axis=1)
    step = pltpu.roll(field, shift_max - 1, axis=1) - near
    near_ref[z, :, :columns] = near
    near_ref[z, :, columns:] = near[:, :lanes]
    step_ref[z, :, :columns] = step
    step_ref[z, :, columns:] = step[:, :lanes]


def sheared(near_ref, step_ref, z, start, width, amount, weight, lane):
    near = near_ref[z, :, pl.ds(start, width + lanes)]
    step = step_ref[z, :, pl.ds(start, width + lanes)]
    return advance(tiles(near + weight * step), amount, lane)


def fused_kernel(
    absorb_hbm, emit_hbm, measured_ref, cam_ref, offs_ref, frac_ref, ga_hbm, ge_hbm,
    ga_ref, ge_ref, absorb_ref, emit_ref,
    near_a, step_a, near_e, step_e, seen_ref, edge_ref, rim_ref, mine_ref, back_ref,
    other, pair, got, sent, ret, give, keep, grad_a, grad_e, sum_a, sum_e,
    sa, ra, sb, rb, sd, rd, sc, rc, s3, r3, sm, si, so,
):
    slices, rows, columns = absorb_ref.shape
    views, count, _, _, piece = mine_ref.shape
    loads = [
        pltpu.make_async_copy(src, dst, si.at[i])
        for i, (src, dst) in enumerate(((absorb_hbm, absorb_ref), (emit_hbm, emit_ref)))
    ]
    for load in loads:
        load.start()
    cameras = measured_ref.shape[0]
    half = count // 2
    me = lax.axis_index("depth")
    lat = lax.axis_index("lat")
    high, low = me // 2, lax.rem(me, 2)
    partner = high * 2 + 1 - low
    near = low == 0
    barrier = pltpu.get_barrier_semaphore()

    def line(p):
        return lax.rem(high + p, half)

    def send(src, dst, send_sem, recv_sem, to):
        return pltpu.make_async_remote_copy(
            src_ref=src, dst_ref=dst, send_sem=send_sem, recv_sem=recv_sem,
            device_id={"depth": to}, device_id_type=MESH,
        )

    for p in range(1, half):
        pl.semaphore_signal(
            barrier, inc=1, device_id={"depth": line(p) * 2 + low}, device_id_type=MESH
        )
    pl.semaphore_signal(barrier, inc=1, device_id={"depth": partner}, device_id_type=MESH)
    pl.semaphore_signal(barrier, inc=1, device_id={"lat": 1 - lat}, device_id_type=MESH)
    def to_pair(v):
        src = mine_ref.at[v, pl.ds((1 - low) * half, half)]
        return send(src, other.at[v], sa.at[v], ra.at[v], partner)

    def to_line(v, p):
        to = line(p)
        return send(pair.at[v, to], got.at[v, high], sb.at[v, p], rb.at[v, p], to * 2 + low)

    def from_line(v, p):
        to = line(p)
        return send(sent.at[v, to], ret.at[v, high], sd.at[v, p], rd.at[v, p], to * 2 + low)

    def from_pair(v):
        dst = back_ref.at[v, pl.ds(low * half, half)]
        return send(give.at[v], dst, sc.at[v], rc.at[v], partner)

    start = pl.multiple_of((low * half + high) * piece, piece)
    images = pltpu.make_async_copy(measured_ref.at[:, :, pl.ds(start, piece)], seen_ref, sm)
    images.start()
    lower = lat == 0
    for load in loads:
        load.wait()
    for z in range(slices):
        fill(absorb_ref, near_a, step_a, z)
        fill(emit_ref, near_e, step_e, z)
        for f, ref in enumerate((absorb_ref, emit_ref)):
            field = ref[z].astype(jnp.float32)
            edge_ref[f, z : z + 1, :] = jnp.where(lower, field[rows - 1 :], field[:1])
    pl.semaphore_wait(barrier, half + 1)
    rim = pltpu.make_async_remote_copy(
        src_ref=edge_ref, dst_ref=rim_ref, send_sem=s3, recv_sem=r3,
        device_id={"lat": 1 - lat}, device_id_type=MESH,
    )
    rim.start()

    def combine(v):
        to_pair(v).wait_recv()
        if v + ahead < views - 1:
            to_pair(v + ahead).start()
        for p in [*range(1, half), 0]:
            h = line(p)
            own_t, own_l = mine_ref[v, low * half + h, 0], mine_ref[v, low * half + h, 1]
            oth_t, oth_l = other[v, h, 0], other[v, h, 1]
            trans = own_t * oth_t
            light = jnp.where(near, own_l + own_t * oth_l, oth_l + oth_t * own_l)
            if p:
                pair[v, h, 0] = trans
                pair[v, h, 1] = light
                to_line(v, p).start()
            else:
                got[v, h, 0] = trans
                got[v, h, 1] = light

    def scan(v):
        for p in range(1, half):
            to_line(v, p).wait_recv()
        fronts = [jnp.ones((rows, piece), jnp.float32)]
        for j in range(half - 1):
            fronts.append(fronts[-1] * got[v, j, 0])
        behind = jnp.zeros((rows, piece), jnp.float32)
        for j in reversed(range(half)):
            sent[v, j, 1] = behind
            behind = got[v, j, 1] + got[v, j, 0] * behind
        adjoint = jnp.zeros((rows, piece), jnp.float32)
        for k in range(cameras):
            seen = jnp.where(cam_ref[0, k] == v, 1.0, 0.0).astype(jnp.float32)
            adjoint += seen * (behind - seen_ref[k])
        for j in range(half):
            sent[v, j, 0] = adjoint * fronts[j]
        for p in range(1, half):
            from_line(v, p).start()
        ret[v, high] = sent[v, high]

    def spread(v):
        for p in range(1, half):
            from_line(v, p).wait_recv()
        for h in range(half):
            at = low * half + h
            own_t, own_l = mine_ref[v, at, 0], mine_ref[v, at, 1]
            oth_t, oth_l = other[v, h, 0], other[v, h, 1]
            front, behind = ret[v, h, 0], ret[v, h, 1]
            give[v, h, 0] = jnp.where(near, front * own_t, front)
            give[v, h, 1] = jnp.where(near, behind, own_l + own_t * behind)
            back_ref[v, at, 0] = jnp.where(near, front, front * oth_t)
            back_ref[v, at, 1] = jnp.where(near, oth_l + oth_t * behind, behind)
        from_pair(v).start()

    lane = lax.broadcasted_iota(jnp.int32, (rows, lanes), 1)
    per = piece // lanes
    wide = 1024

    def forward(v):
        weight = frac_ref[v]

        def chunk_loop(ch, _):
            begin = pl.multiple_of(ch * wide, wide)
            run, light = None, None
            for z in range(slices):
                amount = offs_ref[v, z] + shift_max
                optical = sheared(near_a, step_a, z, begin, wide, amount, weight, lane)
                glowing = sheared(near_e, step_e, z, begin, wide, amount, weight, lane)
                trans = [jnp.exp(-o) for o in optical]
                radiance = [g * (1.0 - t) for g, t in zip(glowing, trans)]
                at = pl.ds(begin, wide)
                keep[v, z, 0, :, at] = jnp.concatenate(trans, axis=1)
                keep[v, z, 1, :, at] = jnp.concatenate(glowing, axis=1)
                if z == 0:
                    run, light = trans, radiance
                else:
                    keep[v, z, 2, :, at] = jnp.concatenate(run, axis=1)
                    light = [l + r * x for l, r, x in zip(light, run, radiance)]
                    run = [r * t for r, t in zip(run, trans)]
            for i in range(wide // lanes):
                dest = ch * (wide // piece) + i // per
                cols = slice((i % per) * lanes, (i % per + 1) * lanes)
                mine_ref[v, dest, 0, :, cols] = run[i]
                mine_ref[v, dest, 1, :, cols] = light[i]
            return 0

        lax.fori_loop(0, columns // wide, chunk_loop, 0)

    def gradient(v, side):
        def piece_loop(h, _):
            p = side * half + h
            at = pl.ds(pl.multiple_of(p * piece, piece), piece)
            front, behind = back_ref[v, p, 0], back_ref[v, p, 1]
            for z in reversed(range(slices)):
                trans, glow = keep[v, z, 0, :, at], keep[v, z, 1, :, at]
                before = front * keep[v, z, 2, :, at] if z else front
                opaque = 1.0 - trans
                grad_e[z, :, at] = before * opaque
                grad_a[z, :, at] = before * trans * (glow - behind)
                behind = glow * opaque + trans * behind
            return 0

        lax.fori_loop(0, half, piece_loop, 0)

    def store(out, z):
        f, dst = (0, ga_hbm) if out is ga_ref else (1, ge_hbm)
        return pltpu.make_async_copy(out.at[z], dst.at[z], so.at[f, z])

    def finish(v):
        from_pair(v).wait_recv()
        gradient(v, 1 - low)
        weight = frac_ref[v]
        for grad in (grad_a, grad_e):
            for z in range(slices):
                grad[z, :, columns:] = grad[z, :, :lanes]

        def slice_loop(z, _):
            amount = shift_max - offs_ref[v, z]
            for grad, total, out in ((grad_a, sum_a, ga_ref), (grad_e, sum_e, ge_ref)):
                near, far = [], []
                for ch in range(columns // wide):
                    parts = tiles(grad[z, :, ch * wide : (ch + 1) * wide + lanes])
                    moved = jnp.concatenate(advance(parts, amount, lane), axis=1)
                    at = slice(ch * wide, (ch + 1) * wide)
                    a, b = (1.0 - weight) * moved, weight * moved
                    if v:
                        a, b = a + total[0, z, :, at], b + total[1, z, :, at]
                    if v < views - 1:
                        total[0, z, :, at] = a
                        total[1, z, :, at] = b
                    near.append(a)
                    far.append(b)
                if v == views - 1:
                    far = pltpu.roll(jnp.concatenate(far, axis=1), 1, axis=1)
                    both = jnp.concatenate(near, axis=1) + far
                    out[z] = out[z] + pltpu.roll(both, shift_max, axis=1)
                    store(out, z).start()
            return 0

        lax.fori_loop(0, slices, slice_loop, 0)

    def smooth(f, field_ref, out, reg):
        row = lax.broadcasted_iota(jnp.int32, (rows, columns), 0)
        col = lax.broadcasted_iota(jnp.int32, (rows, columns), 1)
        for z in range(slices):
            field = field_ref[z].astype(jnp.float32)
            edge = rim_ref[f, z : z + 1, :]
            up = jnp.where(row == 0, jnp.where(lower, 0.0, edge), pltpu.roll(field, 1, axis=0))
            down = jnp.where(
                row == rows - 1, jnp.where(lower, edge, 0.0), pltpu.roll(field, rows - 1, axis=0)
            )
            left = jnp.where(col == 0, 0.0, pltpu.roll(field, 1, axis=1))
            right = jnp.where(col == columns - 1, 0.0, pltpu.roll(field, columns - 1, axis=1))
            out[z] = -reg * (down + up + right + left - 4.0 * field)

    ahead = 2
    for v in range(views - 1):
        forward(v)
        if v < ahead:
            to_pair(v).start()
    images.wait()
    for turn in range(views + 3):
        if turn < views:
            combine(turn)
        if turn == 0:
            forward(views - 1)
        if turn == views - 1 - ahead:
            to_pair(views - 1).start()
        if 0 <= turn - 1 < views:
            scan(turn - 1)
        if turn == 1:
            rim.wait_recv()
            smooth(0, absorb_ref, ga_ref, reg_absorb)
        if 0 <= turn - 2 < views:
            spread(turn - 2)
        if 0 <= turn - 3 < views:
            finish(turn - 3)
        if 0 <= turn - 2 < views:
            gradient(turn - 2, low)
        if turn == 2:
            smooth(1, emit_ref, ge_ref, reg_emit)
    for z in range(slices):
        store(ga_ref, z).wait()
        store(ge_ref, z).wait()
    rim.wait_send()
    for v in range(views):
        to_pair(v).wait_send()
        for p in range(1, half):
            to_line(v, p).wait_send()
            from_line(v, p).wait_send()
        from_pair(v).wait_send()


def body(absorb, emission, measured, camera_view, offsets, fractions):
    slices, rows, columns = absorb.shape
    views, cameras = offsets.shape[0], measured.shape[0]
    count = lax.axis_size("depth")
    half, piece = count // 2, columns // count
    hbm = pl.BlockSpec(memory_space=pltpu.HBM)
    scalar = pl.BlockSpec(memory_space=pltpu.SMEM)
    dma = pltpu.SemaphoreType.DMA

    def room(*shape):
        return pltpu.VMEM(shape, jnp.float32)

    padded = room(slices, rows, columns + lanes)
    return pl.pallas_call(
        fused_kernel,
        out_shape=(
            jax.ShapeDtypeStruct(absorb.shape, jnp.float32),
            jax.ShapeDtypeStruct(absorb.shape, jnp.float32),
        ),
        in_specs=[hbm, hbm, hbm, scalar, scalar, scalar],
        out_specs=(hbm, hbm),
        scratch_shapes=[
            *[room(slices, rows, columns)] * 2,
            *[pltpu.VMEM(absorb.shape, absorb.dtype)] * 2,
            *[padded] * 4,
            room(cameras, rows, piece),
            *[room(2, slices, columns)] * 2,
            *[room(views, count, 2, rows, piece)] * 2,
            *[room(views, half, 2, rows, piece)] * 6,
            room(views, slices, 3, rows, columns),
            *[padded] * 2,
            *[room(2, slices, rows, columns)] * 2,
            *[dma((views,))] * 2, *[dma((views, half))] * 4, *[dma((views,))] * 2,
            dma, dma, dma, dma((2,)), dma((2, slices)),
        ],
        compiler_params=pltpu.CompilerParams(
            vmem_limit_bytes=60 * 1024 * 1024, collective_id=0, has_side_effects=True
        ),
        name="tomography",
    )(absorb, emission, measured, camera_view.T, offsets, fractions)


def solution(mesh):
    placed = (
        P("depth", ("groups", "lat"), None),
        P("depth", ("groups", "lat"), None),
        P(None, ("groups", "lat"), None),
        P(),
        P(None, "depth"),
        P(),
    )
    return jax.shard_map(
        body,
        mesh=mesh,
        in_specs=placed,
        out_specs=(P("depth", ("groups", "lat"), None), P("depth", ("groups", "lat"), None)),
        check_vma=False,
    )
```
